256 devices in a mesh: gx: 8 (over z_lo, y), gy: 4 (over z_hi), gz: 8 (over x, core).
Axes of the slice: x: 4, y: 4, z: 8 (z_hi: 4, z_lo: 2; z = z_hi * 2 + z_lo), core: 2. Of those that a mesh axis runs over, the one named last changes fastest.
Arguments:
- tensor: float32 [1024, 512, 1024], P('gx', 'gy', 'gz'), may hold values from -0.75 to 0.75
- factor_a: float32 [256, 1024], P(('gy', 'gz'), 'gx'), may hold values from -1.7 to 1.7
- factor_b: float32 [256, 512], P(('gx', 'gz'), 'gy'), may hold values from -1.7 to 1.7
- factor_c: float32 [256, 1024], P(('gx', 'gy'), 'gz'), may hold values from -1.7 to 1.7
Outputs:
- grad_a: float32 [256, 1024], P(('gy', 'gz'), 'gx')
- grad_b: float32 [256, 512], P(('gx', 'gz'), 'gy')
- grad_c: float32 [256, 1024], P(('gx', 'gy'), 'gz')
The draws below stay inside these ranges and needn't reach their ends.
All inputs are finite; a program needn't handle non-finite values.
Results may differ from the reference program's by a relative error of at most 0.00019.
Values sent between devices are 32-bit elements; how exact they have to be, the bound alone decides.
A program may use at most 128 MiB of HBM per device.

```python
import jax
import jax.numpy as jnp
from jax import lax

R = 64
S = 4
SR = 256
NI = 1024
NJ = 512
NK = 1024


base_scale = 0.014


def factor_values(key, noise, row_count):
    row_key = jax.random.fold_in(key, 1)
    col_key = jax.random.fold_in(key, 2)
    col_count = noise.shape[0]
    row_scale = jnp.exp(jax.random.uniform(row_key, (row_count,), jnp.float32, -0.5, 0.5) * jnp.log(10.0))
    col_scale = jnp.exp(jax.random.uniform(col_key, (col_count,), jnp.float32, -0.5, 0.5) * jnp.log(10.0))
    rising = 1.0 + 2.0 * jnp.arange(row_count, dtype=jnp.float32) / (row_count - 1)
    return noise * col_scale[:, None] * (row_scale * rising)[None, :] * base_scale


def draw_factor_a(key, part):
    key = jax.random.fold_in(key, 11)
    noise_key = jax.random.fold_in(key, 5)
    noise = jnp.clip(jax.random.normal(noise_key, (SR, NI), jnp.float32), -4.0, 4.0)
    return factor_values(key, noise, NI)


def draw_factor_b(key, part):
    key = jax.random.fold_in(key, 23)
    noise_key = jax.random.fold_in(key, 5)
    noise = jnp.clip(jax.random.normal(noise_key, (SR, NJ), jnp.float32), -4.0, 4.0)
    return factor_values(key, noise, NJ)


def draw_factor_c(key, part):
    key = jax.random.fold_in(key, 37)
    noise_key = jax.random.fold_in(key, 5)
    noise = jnp.clip(jax.random.normal(noise_key, (SR, NK), jnp.float32), -4.0, 4.0)
    return factor_values(key, noise, NK)


def steps_of(key, dims, pieces, low, largest):
    factor_of, own = 1.0, jax.random.fold_in(key, 6)
    for position, parts in pieces:
        heights = jnp.exp(jax.random.uniform(jax.random.fold_in(own, position), (parts,), jnp.float32, low / len(pieces), largest / len(pieces)))
        factor_of = factor_of * jnp.repeat(heights, dims[position] // parts).reshape([-1 if axis == position else 1 for axis in range(len(dims))])
    return factor_of


def centred(rng, dims, scale, limit, shards=(), kind=jnp.bfloat16):
    loudness = steps_of(rng, dims, shards, -0.22, 0.18) if shards else 1.0
    array = jax.random.normal(rng, dims, jnp.float32) * scale * loudness
    return jnp.minimum(jnp.maximum(array, -limit), limit).astype(kind)


def setup_inputs(seed: int = 0) -> dict:
    arg_keys = jax.random.split(jax.random.key(seed), 5)
    return {
        "tensor": centred(arg_keys[0], (NI, NJ, NK), 0.125, 0.75, ((0, 8), (1, 4), (2, 8)), jnp.float32),
        "factor_a": draw_factor_a(jax.random.fold_in(arg_keys[4], 71), 0),
        "factor_b": draw_factor_b(jax.random.fold_in(arg_keys[4], 71), 0),
        "factor_c": draw_factor_c(jax.random.fold_in(arg_keys[4], 71), 0),
    }


exact_mode = lax.Precision.HIGHEST


def block_gram(factor):
    shaped = factor.reshape(S, R, factor.shape[1])
    return jnp.einsum('sri,sti->srt', shaped, shaped, precision=exact_mode)


def scaled_factor(factor, hessian):
    shaped = factor.reshape(S, R, factor.shape[1])
    return jnp.einsum('sri,srt->sti', shaped, hessian, precision=exact_mode).reshape(factor.shape)


def reference(tensor, factor_a, factor_b, factor_c):
    gram_a = block_gram(factor_a)
    gram_b = block_gram(factor_b)
    gram_c = block_gram(factor_c)
    list_a, list_b, list_c = [], [], []
    for start in range(S):
        part_a = factor_a[start * R:(start + 1) * R]
        part_b = factor_b[start * R:(start + 1) * R]
        part_c = factor_c[start * R:(start + 1) * R]
        first_y = jnp.einsum('ijk,cj->cik', tensor, part_b, precision=exact_mode)
        list_a.append(jnp.einsum('cik,ck->ci', first_y, part_c, precision=exact_mode))
        list_c.append(jnp.einsum('cik,ci->ck', first_y, part_a, precision=exact_mode))
        second_y = jnp.einsum('ijk,ck->cij', tensor, part_c, precision=exact_mode)
        list_b.append(jnp.einsum('cij,ci->cj', second_y, part_a, precision=exact_mode))
    m_a = jnp.concatenate(list_a, axis=0)
    m_b = jnp.concatenate(list_b, axis=0)
    m_c = jnp.concatenate(list_c, axis=0)
    grad_a = scaled_factor(factor_a, gram_b * gram_c) - m_a
    grad_b = scaled_factor(factor_b, gram_a * gram_c) - m_b
    grad_c = scaled_factor(factor_c, gram_a * gram_b) - m_c
    return (grad_a, grad_b, grad_c)
```

```python
import functools

import jax
import jax.numpy as jnp
from jax import lax
from jax.experimental import pallas as pl
from jax.experimental.pallas import tpu as pltpu
from jax.sharding import PartitionSpec as P

R = 64
SR = 256
LEN = 128
CHUNKS = 8
STEP = 16
MESH = pl.DeviceIdType.MESH
bf16 = jnp.bfloat16
f32 = jnp.float32


def split(value):
    high = value.astype(bf16)
    return high, (value - high.astype(f32)).astype(bf16)


def stacked(value):
    high, low = split(value)
    return jnp.concatenate([high, high], 0), jnp.concatenate([low, low], 0)


def mm(left, right):
    return jnp.dot(left, right, preferred_element_type=f32)


def wait_bytes(ref, sem):
    pltpu.make_async_copy(ref, ref, sem).wait()


def kernel(
    t_hbm, a_in, b_in, c_in, a_out, b_out, c_out,
    t_in, x_rows, x_cols, ga, gb, gc, wb, wc, a_t, b_t, acc_a, acc_b, acc_c, ha, hb, hc,
    pa, pb, pc, ra, rb, rc, sa, sb, sc, qa, qb, qc,
    t_sem, send, recv,
):
    gx, gy, gz = lax.axis_index("gx"), lax.axis_index("gy"), lax.axis_index("gz")
    z_lo, y = gx // 4, gx % 4

    gy_peers = [(gx, (gy + d) % 4, gz) for d in range(1, 4)]
    gz_peers = [(gx, gy, (gz + d) % 8) for d in range(1, 8)]
    y_peers = [(z_lo * 4 + (y + d) % 4, gy, gz) for d in range(1, 4)]
    lo = 1 - z_lo
    b_peers = [((lo if e else z_lo) * 4 + y, gy, (gz + d) % 8) for e in (0, 1) for d in range(8) if e or d]
    c_peers = [((lo if e else z_lo) * 4 + y, (gy + d) % 4, gz) for e in (0, 1) for d in range(4) if e or d]
    partners = gy_peers + y_peers + b_peers + [p for n, p in enumerate(c_peers) if n >= 4]

    def b_slot(peer):
        return peer[0] // 4 * 8 + peer[2]

    def c_slot(peer):
        return peer[0] // 4 * 4 + peer[1]

    me = (gx, gy, gz)
    b_me, c_me = b_slot(me), c_slot(me)

    def put(src, dst, peer, stage):
        pltpu.make_async_remote_copy(
            src_ref=src, dst_ref=dst, send_sem=send.at[stage], recv_sem=recv.at[stage],
            device_id=peer, device_id_type=MESH,
        ).start()

    per = LEN // CHUNKS

    def t_copy(n):
        rows = pl.ds(n * per, per)
        return pltpu.make_async_copy(t_hbm.at[rows], t_in.at[rows], t_sem.at[n])

    for n in range(CHUNKS):
        t_copy(n).start()

    barrier = pltpu.get_barrier_semaphore()
    for peer in partners:
        pl.semaphore_signal(barrier, inc=1, device_id=peer, device_id_type=MESH)
    ga[gz, gy] = a_in[...]
    gb[y, b_me] = b_in[...]
    gc[y, c_me] = c_in[...]
    pl.semaphore_wait(barrier, len(partners))

    for peer in c_peers:
        put(gc.at[y, c_me], gc.at[y, c_me], peer, 0)
    for peer in b_peers:
        put(gb.at[y, b_me], gb.at[y, b_me], peer, 1)
    for peer in gy_peers:
        put(ga.at[gz, gy], ga.at[gz, gy], peer, 2)

    def prepare(n):
        t_copy(n).wait()

        def body(it, _):
            for u in range(4):
                i = n * per + it * 4 + u
                rows = pl.ds(pl.multiple_of(i * LEN, LEN), LEN)
                value = t_in[i]
                high, low = split(value)
                x_rows[rows, 0:LEN] = high
                x_rows[rows, LEN:] = low
                high, low = split(value.T)
                x_cols[rows, 0:LEN] = high
                x_cols[rows, LEN:] = low
            return 0

        lax.fori_loop(0, per // 4, body, 0)

    for n in range(CHUNKS // 2):
        prepare(n)

    wait_bytes(gc.at[0, 0:7], recv.at[0])
    for peer in y_peers:
        put(gc.at[y], gc.at[y], peer, 3)
    wait_bytes(gb.at[0, 0:15], recv.at[1])
    for peer in y_peers:
        put(gb.at[y], gb.at[y], peer, 4)
    wait_bytes(ga.at[0, 0:3], recv.at[2])
    for peer in gz_peers:
        put(ga.at[gz], ga.at[gz], peer, 5)

    for n in range(CHUNKS // 2, CHUNKS):
        prepare(n)

    wait_bytes(gc.at[0:3], recv.at[3])
    wait_bytes(gb.at[0:3], recv.at[4])
    wait_bytes(ga.at[0:7], recv.at[5])

    def gram(rows, weights):
        left = jnp.concatenate(split(rows), 1)
        return mm(left, weights[0]) + mm(left, weights[1])

    rows_c = jnp.concatenate([gc[n, e * 4:e * 4 + 4].reshape(32, LEN) for e in (0, 1) for n in range(4)], 0)
    cols_c = rows_c.T
    weights_c = stacked(cols_c)
    wc[0], wc[1] = weights_c
    gram_c = gram(rows_c, weights_c)
    rows_b = jnp.concatenate([gb[n, e * 8:e * 8 + 8].reshape(32, LEN) for e in (0, 1) for n in range(4)], 0)
    cols_b = rows_b.T
    b_t[...] = cols_b
    weights_b = stacked(cols_b)
    wb[0], wb[1] = weights_b
    gram_b = gram(rows_b, weights_b)
    rows_a = jnp.concatenate([ga[:, n].reshape(64, LEN) for n in range(4)], 0)
    cols_a = rows_a.T
    a_t[...] = cols_a
    gram_a = gram(rows_a, stacked(cols_a))
    mask = lax.broadcasted_iota(jnp.int32, (SR, SR), 0) // R == lax.broadcasted_iota(jnp.int32, (SR, SR), 1) // R

    def hess_term(cols, left, right):
        high, low = split(jnp.where(mask, left * right, 0.0))
        cols_high, cols_low = split(cols)
        return mm(cols_high, high) + mm(cols_low, high) + mm(cols_high, low)

    ha[...] = hess_term(cols_a, gram_b, gram_c)
    acc_b[...] = hess_term(cols_b, gram_a, gram_c)
    acc_c[...] = hess_term(cols_c, gram_a, gram_b)

    def product(x, w, it):
        rows = x[pl.ds(pl.multiple_of(it * (STEP * LEN), STEP * LEN), STEP * LEN), :]
        return (mm(rows, w[0]) + mm(rows, w[1])).reshape(STEP, LEN, SR)

    def rows_step(it, _):
        value = product(x_rows, wc, it)
        total = acc_b[...]
        other = b_t[...]
        for u in range(STEP):
            i = pl.ds(it * STEP + u, 1)
            total = total - value[u] * a_t[i, :]
            acc_a[i, :] = jnp.sum(value[u] * other, axis=0, keepdims=True)
        acc_b[...] = total
        return 0

    lax.fori_loop(0, LEN // STEP, rows_step, 0)

    part_b = acc_b[...].T
    for e in (0, 1):
        for n in range(4):
            q = (e * 4 + n) * 32
            pb[n, e * 8:e * 8 + 8] = part_b[q:q + 32].reshape(8, 4, LEN)
    for peer in y_peers:
        there = peer[0] % 4
        put(pb.at[there], rb.at[y], peer, 6)
    part_a = (ha[...] - acc_a[...]).T
    for n in range(4):
        pa[:, n] = part_a[n * 64:n * 64 + 64].reshape(8, 8, LEN)
    for peer in gz_peers:
        put(pa.at[peer[2]], ra.at[gz], peer, 7)

    def cols_step(it, _):
        value = product(x_cols, wb, it)
        total = acc_c[...]
        for u in range(STEP):
            total = total - value[u] * a_t[pl.ds(it * STEP + u, 1), :]
        acc_c[...] = total
        return 0

    half = LEN // STEP // 2
    lax.fori_loop(0, half, cols_step, 0)

    wait_bytes(rb.at[0:3], recv.at[6])
    rb[y] = pb[y]
    sb[...] = (rb[0] + rb[1]) + (rb[2] + rb[3])
    for peer in b_peers:
        put(sb.at[b_slot(peer)], qb.at[b_me], peer, 8)
    wait_bytes(ra.at[0:7], recv.at[7])
    ra[gz] = pa[gz]
    sa[...] = ((ra[0] + ra[1]) + (ra[2] + ra[3])) + ((ra[4] + ra[5]) + (ra[6] + ra[7]))
    for peer in gy_peers:
        put(sa.at[peer[1]], qa.at[gy], peer, 9)

    lax.fori_loop(half, 2 * half, cols_step, 0)

    part_c = acc_c[...].T
    for e in (0, 1):
        for n in range(4):
            q = (e * 4 + n) * 32
            pc[n, e * 4:e * 4 + 4] = part_c[q:q + 32].reshape(4, 8, LEN)
    for peer in y_peers:
        put(pc.at[peer[0] % 4], rc.at[y], peer, 10)

    wait_bytes(qb.at[0:15], recv.at[8])
    qb[b_me] = sb[b_me]
    b_out[...] = jnp.sum(qb[...], axis=0)
    wait_bytes(qa.at[0:3], recv.at[9])
    qa[gy] = sa[gy]
    a_out[...] = (qa[0] + qa[1]) + (qa[2] + qa[3])

    wait_bytes(rc.at[0:3], recv.at[10])
    rc[y] = pc[y]
    sc[...] = (rc[0] + rc[1]) + (rc[2] + rc[3])
    for peer in c_peers:
        put(sc.at[c_slot(peer)], qc.at[c_me], peer, 11)
    wait_bytes(qc.at[0:7], recv.at[11])
    qc[c_me] = sc[c_me]
    c_out[...] = jnp.sum(qc[...], axis=0)

    wait_bytes(gc.at[0, 0:7], send.at[0])
    wait_bytes(gb.at[0, 0:15], send.at[1])
    wait_bytes(ga.at[0, 0:3], send.at[2])
    wait_bytes(gc.at[0:3], send.at[3])
    wait_bytes(gb.at[0:3], send.at[4])
    wait_bytes(ga.at[0:7], send.at[5])
    wait_bytes(pb.at[0:3], send.at[6])
    wait_bytes(pa.at[0:7], send.at[7])
    wait_bytes(qb.at[0:15], send.at[8])
    wait_bytes(qa.at[0:3], send.at[9])
    wait_bytes(pc.at[0:3], send.at[10])
    wait_bytes(qc.at[0:7], send.at[11])


def body(tensor, factor_a, factor_b, factor_c):
    vmem = pl.BlockSpec(memory_space=pltpu.VMEM)
    rows = LEN * LEN
    return pl.pallas_call(
        kernel,
        out_shape=[jax.ShapeDtypeStruct(v.shape, f32) for v in (factor_a, factor_b, factor_c)],
        in_specs=[pl.BlockSpec(memory_space=pl.ANY), vmem, vmem, vmem],
        out_specs=[vmem, vmem, vmem],
        scratch_shapes=[
            pltpu.VMEM((LEN, LEN, LEN), f32),
            pltpu.VMEM((rows, 2 * LEN), bf16),
            pltpu.VMEM((rows, 2 * LEN), bf16),
            pltpu.VMEM((8, 4, 8, LEN), f32),
            pltpu.VMEM((4, 16, 4, LEN), f32),
            pltpu.VMEM((4, 8, 8, LEN), f32),
            pltpu.VMEM((2, SR, SR), bf16),
            pltpu.VMEM((2, SR, SR), bf16),
            pltpu.VMEM((LEN, SR), f32),
            pltpu.VMEM((LEN, SR), f32),
            pltpu.VMEM((LEN, SR), f32),
            pltpu.VMEM((LEN, SR), f32),
            pltpu.VMEM((LEN, SR), f32),
            pltpu.VMEM((LEN, SR), f32),
            pltpu.VMEM((LEN, SR), f32),
            pltpu.VMEM((LEN, SR), f32),
            pltpu.VMEM((8, 4, 8, LEN), f32),
            pltpu.VMEM((4, 16, 4, LEN), f32),
            pltpu.VMEM((4, 8, 8, LEN), f32),
            pltpu.VMEM((8, 4, 8, LEN), f32),
            pltpu.VMEM((4, 16, 4, LEN), f32),
            pltpu.VMEM((4, 8, 8, LEN), f32),
            pltpu.VMEM((4, 8, LEN), f32),
            pltpu.VMEM((16, 4, LEN), f32),
            pltpu.VMEM((8, 8, LEN), f32),
            pltpu.VMEM((4, 8, LEN), f32),
            pltpu.VMEM((16, 4, LEN), f32),
            pltpu.VMEM((8, 8, LEN), f32),
            pltpu.SemaphoreType.DMA((CHUNKS,)),
            pltpu.SemaphoreType.DMA((12,)),
            pltpu.SemaphoreType.DMA((12,)),
        ],
        compiler_params=pltpu.CompilerParams(
            collective_id=0, has_side_effects=True, vmem_limit_bytes=56 * 2**20
        ),
    )(tensor, factor_a, factor_b, factor_c)


def solution(mesh):
    in_specs = (
        P("gx", "gy", "gz"),
        P(("gy", "gz"), "gx"),
        P(("gx", "gz"), "gy"),
        P(("gx", "gy"), "gz"),
    )
    out_specs = (P(("gy", "gz"), "gx"), P(("gx", "gz"), "gy"), P(("gx", "gy"), "gz"))
    return jax.shard_map(body, mesh=mesh, in_specs=in_specs, out_specs=out_specs, check_vma=False)
```

```python
import jax
import jax.numpy as jnp
from jax import lax
from jax.experimental import pallas as pl
from jax.experimental.pallas import tpu as pltpu
from jax.sharding import PartitionSpec as P

PH = {"g", "prep", "gram", "l1", "l2", "rs"}
DIRECT = set("gb rb".split())
R = 64
SR = 256
LEN = 128
CHUNKS = 8
STEP = 64
MESH = pl.DeviceIdType.MESH
bf16 = jnp.bfloat16
f32 = jnp.float32


def split(value):
    high = value.astype(bf16)
    return high, (value - high.astype(f32)).astype(bf16)


def stacked(value):
    high, low = split(value)
    return jnp.concatenate([high, high], 0), jnp.concatenate([low, low], 0)


def mm(left, right):
    return jnp.dot(left, right, preferred_element_type=f32)


def offsets(zh=1, zl=1, y=1, x=1, core=1):
    found = [
        (a, b, c, d, e)
        for a in range(zh) for b in range(zl) for c in range(y) for d in range(x) for e in range(core)
    ]

    def hops(o):
        return min(2 * o[0], 8 - 2 * o[0]) + o[1] + min(o[2], 4 - o[2]) + min(o[3], 4 - o[3]) + o[4] * 0.1

    return sorted(found, key=hops, reverse=True)[:-1]


def kernel(
    t_hbm, a_in, b_in, c_in, out,
    t_in, x_rows, x_cols, ga, gb, gc, wb, wc, a_t, c_t, m_a, acc_a, acc_b, acc_c,
    pa, pb, pc, ra, rb, rc, sa, sb, sc, qa, qb, qc,
    t_sem, in_sem, send, recv,
):
    gx, gy, gz = lax.axis_index("gx"), lax.axis_index("gy"), lax.axis_index("gz")
    z_lo, y = gx // 4, gx % 4
    x, core = gz // 2, gz % 2

    def peers(**extent):
        return [
            (((z_lo + b) % 2) * 4 + (y + c) % 4, (gy + a) % 4, ((x + d) % 4) * 2 + (core + e) % 2)
            for a, b, c, d, e in offsets(**extent)
        ]

    def slot_a(d):
        return d[2] * 4 + d[1]

    def slot_b(d):
        return d[0] % 4 * 16 + d[0] // 4 * 8 + d[2]

    def slot_c(d):
        return d[0] % 4 * 8 + d[0] // 4 * 4 + d[1]

    me = (gx, gy, gz)
    me_a, me_b, me_c = slot_a(me), slot_b(me), slot_c(me)
    started = []

    def put(src, dst, peer, stage):
        pltpu.make_async_remote_copy(
            src_ref=src, dst_ref=dst, send_sem=send.at[stage], recv_sem=recv.at[stage],
            device_id=peer, device_id_type=MESH,
        ).start()

    def wait_bytes(ref, count, sem):
        pltpu.make_async_copy(ref.at[0:count], ref.at[0:count], sem).wait()

    def arrived(ref, count, stage):
        wait_bytes(ref, count, recv.at[stage])
        started.append((ref, count, stage))

    class Factor:
        def __init__(self, full, first, second, run, slot, outer, inner, g, p, r, s, q, base, name):
            self.full, self.first, self.second = peers(**full), peers(**first), peers(**second)
            self.run, self.slot, self.outer, self.inner = run, slot, outer, inner
            self.g, self.p, self.r, self.s, self.q = g, p, r, s, q
            self.mine, self.base = slot(me), base
            self.count = len(self.full)
            self.g_direct, self.r_direct = "g" + name in DIRECT, "r" + name in DIRECT

        def runs(self, device):
            return pl.ds(self.outer(device) * self.run, self.run)

        def gather_first(self):
            for peer in self.full if self.g_direct else self.first:
                put(self.g.at[self.mine], self.g.at[self.mine], peer, self.base)

        def gather_second(self):
            if self.g_direct:
                return
            arrived(self.g, len(self.first), self.base)
            block = self.g.at[self.runs(me)]
            for peer in self.second:
                put(block, block, peer, self.base + 1)

        def gather_wait(self):
            if self.g_direct:
                arrived(self.g, self.count, self.base)
            else:
                arrived(self.g, self.run * len(self.second), self.base + 1)

        def reduce_first(self):
            if self.r_direct:
                for peer in self.full:
                    put(self.p.at[self.slot(peer)], self.r.at[self.mine], peer, self.base + 2)
                return
            for peer in self.second:
                put(self.p.at[self.runs(peer)], self.r.at[self.runs(me)], peer, self.base + 2)

        def reduce_second(self):
            if self.r_direct:
                return
            arrived(self.r, self.run * len(self.second), self.base + 2)
            self.r[self.runs(me)] = self.p[self.runs(me)]
            groups = self.r.shape[0] // self.run
            self.s[...] = jnp.sum(self.r[...].reshape(groups, self.run, *self.r.shape[1:]), axis=0)
            for peer in self.first:
                put(self.s.at[self.inner(peer)], self.q.at[self.inner(me)], peer, self.base + 3)

        def reduce_wait(self):
            if self.r_direct:
                arrived(self.r, self.count, self.base + 2)
                self.r[self.mine] = self.p[self.mine]
                return jnp.sum(self.r[...], axis=0)
            arrived(self.q, len(self.first), self.base + 3)
            self.q[self.inner(me)] = self.s[self.inner(me)]
            return jnp.sum(self.q[...], axis=0)

    A = Factor(dict(zh=4, x=4, core=2), dict(zh=4), dict(x=4, core=2), 4, slot_a,
               lambda d: d[2], lambda d: d[1], ga, pa, ra, sa, qa, 0, "a")
    B = Factor(dict(zl=2, y=4, x=4, core=2), dict(zl=2, x=4, core=2), dict(y=4), 16, slot_b,
               lambda d: d[0] % 4, lambda d: d[0] // 4 * 8 + d[2], gb, pb, rb, sb, qb, 4, "b")
    C = Factor(dict(zh=4, zl=2, y=4), dict(zh=4, zl=2), dict(y=4), 8, slot_c,
               lambda d: d[0] % 4, lambda d: d[0] // 4 * 4 + d[1], gc, pc, rc, sc, qc, 8, "c")

    extents = []
    for f, n, one, two, full in (
        ("a", 0, dict(zh=4), dict(x=4, core=2), dict(zh=4, x=4, core=2)),
        ("b", 1, dict(zl=2, x=4, core=2), dict(y=4), dict(zl=2, y=4, x=4, core=2)),
        ("c", 2, dict(zh=4, zl=2), dict(y=4), dict(zh=4, zl=2, y=4)),
    ):
        for kind in "gr":
            extents += [full] if kind + f in DIRECT else [one, two]
    wanted = sorted({o for e in extents for o in offsets(**e)})
    partners = [
        (((z_lo + b) % 2) * 4 + (y + c) % 4, (gy + a) % 4, ((x + d) % 4) * 2 + (core + e) % 2)
        for a, b, c, d, e in wanted
    ]

    per = LEN // CHUNKS

    def t_copy(n):
        rows = pl.ds(n * per, per)
        return pltpu.make_async_copy(t_hbm.at[rows], t_in.at[rows], t_sem.at[n])

    barrier = pltpu.get_barrier_semaphore()
    for peer in partners:
        pl.semaphore_signal(barrier, inc=1, device_id=peer, device_id_type=MESH)
    own = [
        pltpu.make_async_copy(src, dst, in_sem.at[n])
        for n, (src, dst) in enumerate(((a_in, ga.at[me_a]), (b_in, gb.at[me_b]), (c_in, gc.at[me_c])))
    ]
    for copy in own:
        copy.start()
    if "prep" in PH:
        for n in range(CHUNKS):
            t_copy(n).start()
    for copy in own:
        copy.wait()
    pl.semaphore_wait(barrier, len(partners))

    if "g" in PH:
        C.gather_first()
        A.gather_first()
        B.gather_first()

    def prepare(n):
        t_copy(n).wait()

        def body(it, _):
            for u in range(4):
                i = n * per + it * 4 + u
                rows = pl.ds(pl.multiple_of(i * LEN, LEN), LEN)
                value = t_in[i]
                high, low = split(value)
                x_rows[rows, 0:LEN] = high
                x_rows[rows, LEN:] = low
                high, low = split(value.T)
                x_cols[rows, 0:LEN] = high
                x_cols[rows, LEN:] = low
            return 0

        lax.fori_loop(0, per // 4, body, 0)

    if "prep" in PH:
        for n in range(CHUNKS // 2):
            prepare(n)
    if "g" in PH:
        C.gather_second()
        A.gather_second()
        B.gather_second()
    if "prep" in PH:
        for n in range(CHUNKS // 2, CHUNKS):
            prepare(n)

    def gram(rows, weights):
        left = jnp.concatenate(split(rows), 1)
        return mm(left, weights[0]) + mm(left, weights[1])

    def hess_term(cols, left, right):
        mask = (
            lax.broadcasted_iota(jnp.int32, (SR, SR), 0) // R
            == lax.broadcasted_iota(jnp.int32, (SR, SR), 1) // R
        )
        high, low = split(jnp.where(mask, left * right, 0.0))
        cols_high, cols_low = split(cols)
        return mm(cols_high, high) + mm(cols_low, high) + mm(cols_high, low)

    if "g" in PH:
        B.gather_wait()
    if "gram" in PH:
        rows_b = jnp.concatenate(
            [gb[n * 16 + e * 8:n * 16 + e * 8 + 8].reshape(32, LEN) for e in (0, 1) for n in range(4)], 0)
        cols_b = rows_b.T
        weights_b = stacked(cols_b)
        wb[0], wb[1] = weights_b
        gram_b = gram(rows_b, weights_b)
    if "g" in PH:
        A.gather_wait()
    if "gram" in PH:
        rows_a = jnp.concatenate([ga[s * 4 + n] for n in range(4) for s in range(8)], 0)
        cols_a = rows_a.T
        a_t[...] = cols_a
        gram_a = gram(rows_a, stacked(cols_a))
    if "g" in PH:
        C.gather_wait()
    if "gram" in PH:
        rows_c = jnp.concatenate(
            [gc[n * 8 + e * 4:n * 8 + e * 4 + 4].reshape(32, LEN) for e in (0, 1) for n in range(4)], 0)
        cols_c = rows_c.T
        c_t[...] = cols_c
        weights_c = stacked(cols_c)
        wc[0], wc[1] = weights_c
        gram_c = gram(rows_c, weights_c)
        acc_a[...] = hess_term(cols_a, gram_b, gram_c)
        acc_b[...] = hess_term(cols_b, gram_a, gram_c)
        acc_c[...] = hess_term(cols_c, gram_a, gram_b)

    def product(x, w, it):
        rows = x[pl.ds(pl.multiple_of(it * (STEP * LEN), STEP * LEN), STEP * LEN), :]
        return (mm(rows, w[0]) + mm(rows, w[1])).reshape(STEP, LEN, SR)

    def cols_step(it, _):
        value = product(x_cols, wb, it)
        total = acc_c[...]
        other = c_t[...]
        for u in range(STEP):
            i = pl.ds(it * STEP + u, 1)
            total = total - value[u] * a_t[i, :]
            m_a[i, :] = jnp.sum(value[u] * other, axis=0, keepdims=True)
        acc_c[...] = total
        return 0

    if "l1" in PH:
        lax.fori_loop(0, LEN // STEP, cols_step, 0)

    if "rs" in PH:
        part_c = acc_c[...].T
        for e in (0, 1):
            for n in range(4):
                q = (e * 4 + n) * 32
                pc[n * 8 + e * 4:n * 8 + e * 4 + 4] = part_c[q:q + 32].reshape(4, 8, LEN)
        C.reduce_first()
        part_a = (acc_a[...] - m_a[...]).T
        for n in range(4):
            for s in range(8):
                q = n * 64 + s * 8
                pa[s * 4 + n] = part_a[q:q + 8]
        A.reduce_first()

    def rows_step(it, _):
        value = product(x_rows, wc, it)
        total = acc_b[...]
        for u in range(STEP):
            total = total - value[u] * a_t[pl.ds(it * STEP + u, 1), :]
        acc_b[...] = total
        return 0

    if "l2" in PH:
        lax.fori_loop(0, LEN // STEP, rows_step, 0)

    if "rs" in PH:
        part_b = acc_b[...].T
        for e in (0, 1):
            for n in range(4):
                q = (e * 4 + n) * 32
                pb[n * 16 + e * 8:n * 16 + e * 8 + 8] = part_b[q:q + 32].reshape(8, 4, LEN)
        B.reduce_first()
        C.reduce_second()
        A.reduce_second()
        B.reduce_second()
        out[8:16] = C.reduce_wait()
        out[0:8] = A.reduce_wait()
        out[16:20] = B.reduce_wait()
    else:
        out[0:8] = ga[0] + gb[0:2].reshape(8, 128) + gc[0] + acc_a[0:8, 0:128] + acc_b[0:8, 0:128] + acc_c[0:8, 0:128]
        out[8:16] = out[0:8]
        out[16:20] = gb[0]

    for ref, count, stage in started:
        wait_bytes(ref, count, send.at[stage])


def unpack(packed, a_out, b_out, c_out):
    a_out[...] = packed[0:8]
    c_out[...] = packed[8:16]
    b_out[...] = packed[16:20]


def body(tensor, factor_a, factor_b, factor_c):
    vmem = pl.BlockSpec(memory_space=pltpu.VMEM)
    blocks = [(32, 8, LEN), (64, 4, LEN), (32, 8, LEN)]
    parts = [(4, 8, LEN), (16, 4, LEN), (8, 8, LEN)]
    packed = pl.pallas_call(
        kernel,
        out_shape=jax.ShapeDtypeStruct((24, LEN), f32),
        in_specs=[pl.BlockSpec(memory_space=pl.ANY)] * 4,
        out_specs=vmem,
        scratch_shapes=[
            pltpu.VMEM((LEN, LEN, LEN), f32),
            pltpu.VMEM((LEN * LEN, 2 * LEN), bf16),
            pltpu.VMEM((LEN * LEN, 2 * LEN), bf16),
            *[pltpu.VMEM(shape, f32) for shape in blocks],
            pltpu.VMEM((2, SR, SR), bf16),
            pltpu.VMEM((2, SR, SR), bf16),
            *[pltpu.VMEM((LEN, SR), f32) for _ in range(6)],
            *[pltpu.VMEM(shape, f32) for shape in blocks],
            *[pltpu.VMEM(shape, f32) for shape in blocks],
            *[pltpu.VMEM(shape, f32) for shape in parts],
            *[pltpu.VMEM(shape, f32) for shape in parts],
            pltpu.SemaphoreType.DMA((CHUNKS,)),
            pltpu.SemaphoreType.DMA((3,)),
            pltpu.SemaphoreType.DMA((12,)),
            pltpu.SemaphoreType.DMA((12,)),
        ],
        compiler_params=pltpu.CompilerParams(
            collective_id=0, has_side_effects=True, vmem_limit_bytes=56 * 2**20
        ),
    )(tensor, factor_a, factor_b, factor_c)
    if not True:
        return packed[0:8], packed[16:20], packed[8:16]
    return pl.pallas_call(
        unpack,
        out_shape=[jax.ShapeDtypeStruct(v.shape, f32) for v in (factor_a, factor_b, factor_c)],
        in_specs=[vmem],
        out_specs=[vmem, vmem, vmem],
    )(packed)


def solution(mesh):
    in_specs = (
        P("gx", "gy", "gz"),
        P(("gy", "gz"), "gx"),
        P(("gx", "gz"), "gy"),
        P(("gx", "gy"), "gz"),
    )
    out_specs = (P(("gy", "gz"), "gx"), P(("gx", "gz"), "gy"), P(("gx", "gy"), "gz"))
    return jax.shard_map(body, mesh=mesh, in_specs=in_specs, out_specs=out_specs, check_vma=False)
```

```python
import jax
import jax.numpy as jnp
from jax import lax
from jax.experimental import pallas as pl
from jax.experimental.pallas import tpu as pltpu
from jax.sharding import PartitionSpec as P

R = 64
SR = 256
LEN = 128
CHUNKS = 8
STEP = 64
MESH = pl.DeviceIdType.MESH
bf16 = jnp.bfloat16
f32 = jnp.float32


def split(value):
    high = value.astype(bf16)
    return high, (value - high.astype(f32)).astype(bf16)


def stacked(value):
    high, low = split(value)
    return jnp.concatenate([high, high], 0), jnp.concatenate([low, low], 0)


def mm(left, right):
    return jnp.dot(left, right, preferred_element_type=f32)


def offsets(zh=1, zl=1, y=1, x=1, core=1):
    found = [
        (a, b, c, d, e)
        for a in range(zh) for b in range(zl) for c in range(y) for d in range(x) for e in range(core)
    ]

    def hops(o):
        return min(2 * o[0], 8 - 2 * o[0]) + o[1] + min(o[2], 4 - o[2]) + min(o[3], 4 - o[3]) + o[4] * 0.1

    return sorted(found, key=hops, reverse=True)[:-1]


def kernel(
    t_hbm, a_in, b_in, c_in, out,
    t_in, x_rows, x_cols, wb, wc, a_t, c_t, m_a, acc_a, acc_b, acc_c,
    ga, gb, gc, pa, pb, pc, ra, rb, rc, sa, sc, qa, qc,
    t_sem, in_sem, send, recv,
):
    gx, gy, gz = lax.axis_index("gx"), lax.axis_index("gy"), lax.axis_index("gz")
    z_lo, y = gx // 4, gx % 4
    x, core = gz // 2, gz % 2
    me = (gx, gy, gz)

    def peer_of(o):
        a, b, c, d, e = o
        return ((z_lo + b) % 2) * 4 + (y + c) % 4, (gy + a) % 4, ((x + d) % 4) * 2 + (core + e) % 2

    def put(src, dst, peer, stage):
        pltpu.make_async_remote_copy(
            src_ref=src, dst_ref=dst, send_sem=send.at[stage], recv_sem=recv.at[stage],
            device_id=peer, device_id_type=MESH,
        ).start()

    def wait_bytes(ref, sem):
        pltpu.make_async_copy(ref, ref, sem).wait()

    started = []

    def arrived(ref, stage):
        wait_bytes(ref, recv.at[stage])
        started.append((ref, stage))

    def at_x(d, e):
        return ((x + d) % 4) * 2 + (core + e) % 2

    gz_peers = [(gx, gy, at_x(d, e)) for d, e in ((2, 1), (2, 0), (1, 1), (3, 1), (1, 0), (3, 0), (0, 1))]
    y_peers = [(z_lo * 4 + (y + c) % 4, gy, gz) for c in (2, 1, 3)]
    a_far = [(gx, (gy + 2) % 4, gz)]
    a_near = [(gx, (gy + a) % 4, gz) for a in (1, 3)]

    def at_z(a, b):
        if b == 0:
            return gx, (gy + a) % 4, gz
        return (1 - z_lo) * 4 + y, (gy + a * (1 - 2 * z_lo) + 8) % 4, gz

    c_far = [at_z(2, 0), at_z(1, 1), at_z(2, 1)]
    c_near = [at_z(1, 0), at_z(3, 0), at_z(0, 1), at_z(3, 1)]
    b_first = [peer_of(o) for o in offsets(zl=2, y=4)]
    b_full = [peer_of(o) for o in offsets(zl=2, y=4, x=4, core=2)]
    partners = a_far + [at_z(2, 1), at_z(1, 1)] + a_near + [at_z(3, 1)] + b_full

    def block_a(ref, d):
        return ref.at[d[1], d[2]]

    def block_b(ref, d):
        return ref.at[d[0], d[2]]

    def block_c(ref, d):
        return ref.at[d[0] // 4, d[0] % 4, d[1]]

    def send_block(block, ref, device, peers, stage):
        for peer in peers:
            put(block(ref, device), block(ref, device), peer, stage)

    per = LEN // CHUNKS

    def t_copy(n):
        rows = pl.ds(n * per, per)
        return pltpu.make_async_copy(t_hbm.at[rows], t_in.at[rows], t_sem.at[n])

    barrier = pltpu.get_barrier_semaphore()
    for peer in partners:
        pl.semaphore_signal(barrier, inc=1, device_id=peer, device_id_type=MESH)
    own = [
        pltpu.make_async_copy(src, dst, in_sem.at[n])
        for n, (src, dst) in enumerate(((a_in, block_a(ga, me)), (b_in, block_b(gb, me)), (c_in, block_c(gc, me))))
    ]
    for copy in own:
        copy.start()
    for n in range(CHUNKS):
        t_copy(n).start()
    for copy in own:
        copy.wait()
    pl.semaphore_wait(barrier, len(partners))

    send_block(block_c, gc, me, c_far, 0)
    send_block(block_a, ga, me, a_far, 2)
    send_block(block_c, gc, me, c_near, 1)
    send_block(block_a, ga, me, a_near, 3)
    send_block(block_b, gb, me, b_first, 4)
    send_block(block_c, gc, me, y_peers, 5)
    send_block(block_a, ga, me, gz_peers, 6)

    def prepare(first, last):
        for n in range(first, last):
            t_copy(n).wait()

            def body(it, _):
                for u in range(4):
                    i = n * per + it * 4 + u
                    rows = pl.ds(pl.multiple_of(i * LEN, LEN), LEN)
                    value = t_in[i]
                    high, low = split(value)
                    x_rows[rows, 0:LEN] = high
                    x_rows[rows, LEN:] = low
                    high, low = split(value.T)
                    x_cols[rows, 0:LEN] = high
                    x_cols[rows, LEN:] = low
                return 0

            lax.fori_loop(0, per // 4, body, 0)

    prepare(0, 5)
    arrived(sc.at[0:4], 1)
    for device in c_near:
        send_block(block_c, gc, device, y_peers, 5)
    arrived(sa.at[0:2], 3)
    for device in a_near:
        send_block(block_a, ga, device, gz_peers, 6)
    prepare(5, 6)
    arrived(gb.at[0, 0:7], 4)
    for peer in gz_peers:
        put(gb.at[:, gz], gb.at[:, gz], peer, 7)
    prepare(6, 7)
    arrived(sc.at[0:3], 0)
    for device in c_far:
        send_block(block_c, gc, device, y_peers, 5)
    arrived(sa.at[0:1], 2)
    for device in a_far:
        send_block(block_a, ga, device, gz_peers, 6)
    prepare(7, 8)

    def gram(rows, weights):
        left = jnp.concatenate(split(rows), 1)
        return mm(left, weights[0]) + mm(left, weights[1])

    def hess(left, right):
        mask = (
            lax.broadcasted_iota(jnp.int32, (SR, SR), 0) // R
            == lax.broadcasted_iota(jnp.int32, (SR, SR), 1) // R
        )
        return split(jnp.where(mask, left * right, 0.0))

    def hess_term(cols, hessian):
        high, low = hessian
        cols_high, cols_low = split(cols)
        return mm(cols_high, high) + mm(cols_low, high) + mm(cols_high, low)

    arrived(gb.at[0:7], 7)
    rows_b = gb[...].reshape(SR, LEN)
    cols_b = rows_b.T
    weights_b = stacked(cols_b)
    wb[0], wb[1] = weights_b
    gram_b = gram(rows_b, weights_b)
    arrived(ra.at[0:7], 6)
    rows_a = ga[...].reshape(SR, LEN)
    cols_a = rows_a.T
    a_t[...] = cols_a
    gram_a = gram(rows_a, stacked(cols_a))
    hess_c = hess(gram_a, gram_b)
    arrived(rc.at[0:3], 5)
    rows_c = gc[...].reshape(SR, LEN)
    cols_c = rows_c.T
    c_t[...] = cols_c
    weights_c = stacked(cols_c)
    wc[0], wc[1] = weights_c
    gram_c = gram(rows_c, weights_c)
    acc_a[...] = hess_term(cols_a, hess(gram_b, gram_c))
    acc_b[...] = hess_term(cols_b, hess(gram_a, gram_c))
    acc_c[...] = hess_term(cols_c, hess_c)

    def product(x, w, it):
        rows = x[pl.ds(pl.multiple_of(it * (STEP * LEN), STEP * LEN), STEP * LEN), :]
        return (mm(rows, w[0]) + mm(rows, w[1])).reshape(STEP, LEN, SR)

    def cols_step(it, _):
        value = product(x_cols, wb, it)
        total = acc_c[...]
        other = c_t[...]
        for u in range(STEP):
            i = pl.ds(it * STEP + u, 1)
            total = total - value[u] * a_t[i, :]
            m_a[i, :] = jnp.sum(value[u] * other, axis=0, keepdims=True)
        acc_c[...] = total
        return 0

    lax.fori_loop(0, LEN // STEP, cols_step, 0)

    def slot_c(d):
        return d[0] // 4 * 4 + d[1]

    pc[...] = acc_c[...].T.reshape(pc.shape)
    for peer in y_peers:
        put(pc.at[:, peer[0] % 4], rc.at[y], peer, 8)
    pa[...] = (acc_a[...] - m_a[...]).T.reshape(pa.shape)
    for peer in gz_peers:
        put(pa.at[:, peer[2]], ra.at[gz], peer, 9)

    def rows_step(it, _):
        value = product(x_rows, wc, it)
        total = acc_b[...]
        for u in range(STEP):
            total = total - value[u] * a_t[pl.ds(it * STEP + u, 1), :]
        acc_b[...] = total
        return 0

    lax.fori_loop(0, LEN // STEP, rows_step, 0)

    pb[...] = acc_b[...].T.reshape(pb.shape)
    for peer in b_full:
        put(block_b(pb, peer), rb.at[gx * 8 + gz], peer, 10)
    arrived(rc.at[0:3], 8)
    rc[y] = pc[:, y]
    sc[...] = ((rc[0] + rc[1]) + (rc[2] + rc[3])).reshape(sc.shape)
    for peer in c_far + c_near:
        put(sc.at[slot_c(peer)], qc.at[slot_c(me)], peer, 11)
    arrived(ra.at[0:7], 9)
    ra[gz] = pa[:, gz]
    sa[...] = ((ra[0] + ra[1]) + (ra[2] + ra[3])) + ((ra[4] + ra[5]) + (ra[6] + ra[7]))
    for peer in a_far + a_near:
        put(sa.at[peer[1]], qa.at[gy], peer, 12)
    arrived(sc.at[0:7], 11)
    qc[slot_c(me)] = sc[slot_c(me)]
    out[8:16] = jnp.sum(qc[...], axis=0)
    arrived(sa.at[0:3], 12)
    qa[gy] = sa[gy]
    out[0:8] = (qa[0] + qa[1]) + (qa[2] + qa[3])
    arrived(rb.at[0:63], 10)
    rb[gx * 8 + gz] = pb[gx, gz]
    out[16:20] = jnp.sum(rb[...], axis=0)

    for ref, stage in started:
        wait_bytes(ref, send.at[stage])


def unpack(packed, a_out, b_out, c_out):
    a_out[...] = packed[0:8]
    c_out[...] = packed[8:16]
    b_out[...] = packed[16:20]


def body(tensor, factor_a, factor_b, factor_c):
    vmem = pl.BlockSpec(memory_space=pltpu.VMEM)
    blocks = [(4, 8, 8, LEN), (8, 8, 4, LEN), (2, 4, 4, 8, LEN)]
    slots = [(8, 4, 8, LEN), (64, 4, LEN), (4, 2, 4, 8, LEN)]
    parts = [(4, 8, LEN), (8, 8, LEN)]
    packed = pl.pallas_call(
        kernel,
        out_shape=jax.ShapeDtypeStruct((24, LEN), f32),
        in_specs=[pl.BlockSpec(memory_space=pl.ANY)] * 4,
        out_specs=vmem,
        scratch_shapes=[
            pltpu.VMEM((LEN, LEN, LEN), f32),
            pltpu.VMEM((LEN * LEN, 2 * LEN), bf16),
            pltpu.VMEM((LEN * LEN, 2 * LEN), bf16),
            pltpu.VMEM((2, SR, SR), bf16),
            pltpu.VMEM((2, SR, SR), bf16),
            *[pltpu.VMEM((LEN, SR), f32) for _ in range(6)],
            *[pltpu.VMEM(shape, f32) for shape in blocks + blocks + slots + parts + parts],
            pltpu.SemaphoreType.DMA((CHUNKS,)),
            pltpu.SemaphoreType.DMA((3,)),
            pltpu.SemaphoreType.DMA((13,)),
            pltpu.SemaphoreType.DMA((13,)),
        ],
        compiler_params=pltpu.CompilerParams(
            collective_id=0, has_side_effects=True, vmem_limit_bytes=56 * 2**20
        ),
    )(tensor, factor_a, factor_b, factor_c)
    if not True:
        return packed[0:8], packed[16:20], packed[8:16]
    return pl.pallas_call(
        unpack,
        out_shape=[jax.ShapeDtypeStruct(v.shape, f32) for v in (factor_a, factor_b, factor_c)],
        in_specs=[vmem],
        out_specs=[vmem, vmem, vmem],
    )(packed)


def solution(mesh):
    in_specs = (
        P("gx", "gy", "gz"),
        P(("gy", "gz"), "gx"),
        P(("gx", "gz"), "gy"),
        P(("gx", "gy"), "gz"),
    )
    out_specs = (P(("gy", "gz"), "gx"), P(("gx", "gz"), "gy"), P(("gx", "gy"), "gz"))
    return jax.shard_map(body, mesh=mesh, in_specs=in_specs, out_specs=out_specs, check_vma=False)
```

```python
import jax
import jax.numpy as jnp
from jax import lax
from jax.experimental import pallas as pl
from jax.experimental.pallas import tpu as pltpu
from jax.sharding import PartitionSpec as P

R = 64
SR = 256
LEN = 128
CHUNKS = 8
STEP = 64
MESH = pl.DeviceIdType.MESH
bf16 = jnp.bfloat16
f32 = jnp.float32


def split(value):
    high = value.astype(bf16)
    return high, (value - high.astype(f32)).astype(bf16)


def stacked(value):
    high, low = split(value)
    return jnp.concatenate([high, high], 0), jnp.concatenate([low, low], 0)


def mm(left, right):
    return jnp.dot(left, right, preferred_element_type=f32)


def offsets(zh=1, zl=1, y=1, x=1, core=1):
    found = [
        (a, b, c, d, e)
        for a in range(zh) for b in range(zl) for c in range(y) for d in range(x) for e in range(core)
    ]

    def hops(o):
        return min(2 * o[0], 8 - 2 * o[0]) + o[1] + min(o[2], 4 - o[2]) + min(o[3], 4 - o[3]) + o[4] * 0.1

    return sorted(found, key=hops, reverse=True)[:-1]


def kernel(
    t_hbm, a_in, b_in, c_in, out,
    t_in, x_rows, x_cols, wb, wc, a_t, c_t, m_a, acc_a, acc_b, acc_c,
    ga, gb, gc, pa, pb, pc, ra, rb, rc, sa, sc, qa, qc,
    t_sem, in_sem, send, recv,
):
    gx, gy, gz = lax.axis_index("gx"), lax.axis_index("gy"), lax.axis_index("gz")
    z_lo, y = gx // 4, gx % 4
    x, core = gz // 2, gz % 2
    me = (gx, gy, gz)

    def peer_of(o):
        a, b, c, d, e = o
        return ((z_lo + b) % 2) * 4 + (y + c) % 4, (gy + a) % 4, ((x + d) % 4) * 2 + (core + e) % 2

    def put(src, dst, peer, stage):
        pltpu.make_async_remote_copy(
            src_ref=src, dst_ref=dst, send_sem=send.at[stage], recv_sem=recv.at[stage],
            device_id=peer, device_id_type=MESH,
        ).start()

    def wait_bytes(ref, sem):
        pltpu.make_async_copy(ref, ref, sem).wait()

    started = []

    def arrived(ref, stage):
        wait_bytes(ref, recv.at[stage])
        started.append((ref, stage))

    def at_x(d, e):
        return ((x + d) % 4) * 2 + (core + e) % 2

    gz_peers = [(gx, gy, at_x(d, e)) for d, e in ((2, 1), (2, 0), (1, 1), (3, 1), (1, 0), (3, 0), (0, 1))]
    y_peers = [(z_lo * 4 + (y + c) % 4, gy, gz) for c in (2, 1, 3)]
    a_far = [(gx, (gy + 2) % 4, gz)]
    a_near = [(gx, (gy + a) % 4, gz) for a in (1, 3)]

    def at_z(a, b):
        if b == 0:
            return gx, (gy + a) % 4, gz
        return (1 - z_lo) * 4 + y, (gy + a * (1 - 2 * z_lo) + 8) % 4, gz

    c_far = [at_z(2, 0), at_z(1, 1), at_z(2, 1)]
    c_near = [at_z(1, 0), at_z(3, 0), at_z(0, 1), at_z(3, 1)]
    b_first = [peer_of(o) for o in offsets(zl=2, y=4)]
    b_full = [peer_of(o) for o in offsets(zl=2, y=4, x=4, core=2)]
    partners = a_far + [at_z(2, 1), at_z(1, 1)] + a_near + [at_z(3, 1)] + b_full

    def block_a(ref, d):
        return ref.at[d[1], d[2]]

    def block_b(ref, d):
        return ref.at[d[0], d[2]]

    def block_c(ref, d):
        return ref.at[d[0] // 4, d[0] % 4, d[1]]

    def send_block(block, ref, device, peers, stage):
        for peer in peers:
            put(block(ref, device), block(ref, device), peer, stage)

    per = LEN // CHUNKS

    def t_copy(n):
        rows = pl.ds(n * per, per)
        return pltpu.make_async_copy(t_hbm.at[rows], t_in.at[rows], t_sem.at[n])

    barrier = pltpu.get_barrier_semaphore()
    for peer in partners:
        pl.semaphore_signal(barrier, inc=1, device_id=peer, device_id_type=MESH)
    own = [
        pltpu.make_async_copy(src, dst, in_sem.at[n])
        for n, (src, dst) in enumerate(((a_in, block_a(ga, me)), (b_in, block_b(gb, me)), (c_in, block_c(gc, me))))
    ]
    for copy in own:
        copy.start()
    for n in range(CHUNKS):
        t_copy(n).start()
    for copy in own:
        copy.wait()
    pl.semaphore_wait(barrier, len(partners))

    send_block(block_c, gc, me, c_far, 0)
    send_block(block_a, ga, me, a_far, 2)
    send_block(block_c, gc, me, c_near, 1)
    send_block(block_a, ga, me, a_near, 3)
    send_block(block_b, gb, me, b_first, 4)
    send_block(block_c, gc, me, y_peers, 5)
    send_block(block_a, ga, me, gz_peers, 6)

    def prepare(first, last):
        for n in range(first, last):
            t_copy(n).wait()

            def body(it, _):
                for u in range(4):
                    i = n * per + it * 4 + u
                    rows = pl.ds(pl.multiple_of(i * LEN, LEN), LEN)
                    value = t_in[i]
                    high, low = split(value)
                    x_rows[rows, 0:LEN] = high
                    x_rows[rows, LEN:] = low
                    high, low = split(value.T)
                    x_cols[rows, 0:LEN] = high
                    x_cols[rows, LEN:] = low
                return 0

            lax.fori_loop(0, per // 4, body, 0)

    prepare(0, 5)
    arrived(sc.at[0:4], 1)
    for device in c_near:
        send_block(block_c, gc, device, y_peers, 5)
    arrived(sa.at[0:2], 3)
    for device in a_near:
        send_block(block_a, ga, device, gz_peers, 6)
    prepare(5, 6)
    arrived(gb.at[0, 0:7], 4)
    for peer in gz_peers:
        put(gb.at[:, gz], gb.at[:, gz], peer, 7)
    prepare(6, 7)
    arrived(sc.at[0:3], 0)
    for device in c_far:
        send_block(block_c, gc, device, y_peers, 5)
    arrived(sa.at[0:1], 2)
    for device in a_far:
        send_block(block_a, ga, device, gz_peers, 6)
    prepare(7, 8)

    def gram(rows, weights):
        left = jnp.concatenate(split(rows), 1)
        return mm(left, weights[0]) + mm(left, weights[1])

    def hess(left, right):
        mask = (
            lax.broadcasted_iota(jnp.int32, (SR, SR), 0) // R
            == lax.broadcasted_iota(jnp.int32, (SR, SR), 1) // R
        )
        return split(jnp.where(mask, left * right, 0.0))

    def hess_term(cols, hessian):
        high, low = hessian
        cols_high, cols_low = split(cols)
        return mm(cols_high, high) + mm(cols_low, high) + mm(cols_high, low)

    arrived(gb.at[0:7], 7)
    rows_b = gb[...].reshape(SR, LEN)
    cols_b = rows_b.T
    weights_b = stacked(cols_b)
    wb[0], wb[1] = weights_b
    gram_b = gram(rows_b, weights_b)
    arrived(ra.at[0:7], 6)
    rows_a = ga[...].reshape(SR, LEN)
    cols_a = rows_a.T
    a_t[...] = cols_a
    gram_a = gram(rows_a, stacked(cols_a))
    hess_c = hess(gram_a, gram_b)
    arrived(rc.at[0:3], 5)
    rows_c = gc[...].reshape(SR, LEN)
    cols_c = rows_c.T
    c_t[...] = cols_c
    weights_c = stacked(cols_c)
    wc[0], wc[1] = weights_c
    gram_c = gram(rows_c, weights_c)
    acc_a[...] = hess_term(cols_a, hess(gram_b, gram_c))
    acc_b[...] = hess_term(cols_b, hess(gram_a, gram_c))
    acc_c[...] = hess_term(cols_c, hess_c)

    def product(x, w, it):
        rows = x[pl.ds(pl.multiple_of(it * (STEP * LEN), STEP * LEN), STEP * LEN), :]
        return (mm(rows, w[0]) + mm(rows, w[1])).reshape(STEP, LEN, SR)

    def cols_step(it, _):
        value = product(x_cols, wb, it)
        total = acc_c[...]
        other = c_t[...]
        for u in range(STEP):
            i = pl.ds(it * STEP + u, 1)
            total = total - value[u] * a_t[i, :]
            m_a[i, :] = jnp.sum(value[u] * other, axis=0, keepdims=True)
        acc_c[...] = total
        return 0

    lax.fori_loop(0, LEN // STEP, cols_step, 0)

    def slot_c(d):
        return d[0] // 4 * 4 + d[1]

    pc[...] = acc_c[...].T.reshape(pc.shape)
    for peer in y_peers:
        put(pc.at[:, peer[0] % 4], rc.at[y], peer, 8)
    pa[...] = (acc_a[...] - m_a[...]).T.reshape(pa.shape)
    for peer in gz_peers:
        put(pa.at[:, peer[2]], ra.at[gz], peer, 9)

    def rows_step(it, _):
        value = product(x_rows, wc, it)
        total = acc_b[...]
        for u in range(STEP):
            total = total - value[u] * a_t[pl.ds(it * STEP + u, 1), :]
        acc_b[...] = total
        return 0

    lax.fori_loop(0, LEN // STEP, rows_step, 0)

    arrived(rc.at[0:3], 8)
    rc[y] = pc[:, y]
    sc[...] = ((rc[0] + rc[1]) + (rc[2] + rc[3])).reshape(sc.shape)
    for peer in c_far + c_near:
        put(sc.at[slot_c(peer)], qc.at[slot_c(me)], peer, 11)
    arrived(ra.at[0:7], 9)
    ra[gz] = pa[:, gz]
    sa[...] = ((ra[0] + ra[1]) + (ra[2] + ra[3])) + ((ra[4] + ra[5]) + (ra[6] + ra[7]))
    for peer in a_far + a_near:
        put(sa.at[peer[1]], qa.at[gy], peer, 12)
    pb[...] = acc_b[...].T.reshape(pb.shape)
    for peer in b_full:
        put(block_b(pb, peer), rb.at[gx * 8 + gz], peer, 10)
    arrived(sc.at[0:7], 11)
    qc[slot_c(me)] = sc[slot_c(me)]
    out[8:16] = jnp.sum(qc[...], axis=0)
    arrived(sa.at[0:3], 12)
    qa[gy] = sa[gy]
    out[0:8] = (qa[0] + qa[1]) + (qa[2] + qa[3])
    arrived(rb.at[0:63], 10)
    rb[gx * 8 + gz] = pb[gx, gz]
    out[16:20] = jnp.sum(rb[...], axis=0)

    for ref, stage in started:
        wait_bytes(ref, send.at[stage])


def unpack(packed, a_out, b_out, c_out):
    a_out[...] = packed[0:8]
    c_out[...] = packed[8:16]
    b_out[...] = packed[16:20]


def body(tensor, factor_a, factor_b, factor_c):
    vmem = pl.BlockSpec(memory_space=pltpu.VMEM)
    blocks = [(4, 8, 8, LEN), (8, 8, 4, LEN), (2, 4, 4, 8, LEN)]
    slots = [(8, 4, 8, LEN), (64, 4, LEN), (4, 2, 4, 8, LEN)]
    parts = [(4, 8, LEN), (8, 8, LEN)]
    packed = pl.pallas_call(
        kernel,
        out_shape=jax.ShapeDtypeStruct((24, LEN), f32),
        in_specs=[pl.BlockSpec(memory_space=pl.ANY)] * 4,
        out_specs=vmem,
        scratch_shapes=[
            pltpu.VMEM((LEN, LEN, LEN), f32),
            pltpu.VMEM((LEN * LEN, 2 * LEN), bf16),
            pltpu.VMEM((LEN * LEN, 2 * LEN), bf16),
            pltpu.VMEM((2, SR, SR), bf16),
            pltpu.VMEM((2, SR, SR), bf16),
            *[pltpu.VMEM((LEN, SR), f32) for _ in range(6)],
            *[pltpu.VMEM(shape, f32) for shape in blocks + blocks + slots + parts + parts],
            pltpu.SemaphoreType.DMA((CHUNKS,)),
            pltpu.SemaphoreType.DMA((3,)),
            pltpu.SemaphoreType.DMA((13,)),
            pltpu.SemaphoreType.DMA((13,)),
        ],
        compiler_params=pltpu.CompilerParams(
            collective_id=0, has_side_effects=True, vmem_limit_bytes=56 * 2**20
        ),
    )(tensor, factor_a, factor_b, factor_c)
    if not True:
        return packed[0:8], packed[16:20], packed[8:16]
    return pl.pallas_call(
        unpack,
        out_shape=[jax.ShapeDtypeStruct(v.shape, f32) for v in (factor_a, factor_b, factor_c)],
        in_specs=[vmem],
        out_specs=[vmem, vmem, vmem],
    )(packed)


def solution(mesh):
    in_specs = (
        P("gx", "gy", "gz"),
        P(("gy", "gz"), "gx"),
        P(("gx", "gz"), "gy"),
        P(("gx", "gy"), "gz"),
    )
    out_specs = (P(("gy", "gz"), "gx"), P(("gx", "gz"), "gy"), P(("gx", "gy"), "gz"))
    return jax.shard_map(body, mesh=mesh, in_specs=in_specs, out_specs=out_specs, check_vma=False)
```
